32 devices in a mesh: groups: 2 (over y), gx: 4 (over z), gy: 4 (over x, core).
Axes of the slice: x: 2, y: 2, z: 4, core: 2. Of those that a mesh axis runs over, the one named last changes fastest.
Arguments:
- states: bfloat16 [48, 2, 8192], P('groups', None, 'gx'), parts along dimension 0, may hold values from -24 to 24
- lengths: int32 [48], P(('groups', 'gx')), parts along dimension 0, may hold values from 1 to 128, 1536 in all
- attn_gain: float32 [8192], P('gx'), may hold values from 0.25 to 1.75
- mlp_gain: float32 [8192], P('gx'), may hold values from 0.25 to 1.75
- w_qkv: bfloat16 [8192, 8, 1280], P('gx', 'gy'), may hold values from -0.0625 to 0.0625
- b_qkv: bfloat16 [8, 1280], P('gy'), may hold values from -3 to 3
- key_cache: bfloat16 [48, 128, 8, 128], P(('groups', 'gx'), None, 'gy'), parts along dimension 0, may hold values from -256 to 256
- value_cache: bfloat16 [48, 128, 8, 128], P(('groups', 'gx'), None, 'gy'), parts along dimension 0, may hold values from -6 to 6
- w_out: bfloat16 [8, 1024, 8192], P('gy', None, 'gx'), may hold values from -0.0625 to 0.0625
- w_gate_up: bfloat16 [8192, 2, 15360], P('gx', None, 'gy'), may hold values from -0.0625 to 0.0625
- w_down: bfloat16 [15360, 8192], P('gy', 'gx'), may hold values from -0.046875 to 0.046875
Outputs:
- layer_out: float32 [48, 2, 8192], P('groups', None, 'gx'), parts along dimension 0
The draws below stay inside these ranges and needn't reach their ends.
There are 2 independent parts, one for each index of `groups`. The reference program is written for one: setup_inputs(seed, part) draws one part's arguments, and reference() takes and returns one part's arrays. A program takes and returns all parts, laid end to end along the dimension named above; an argument that names none is the same for every part. Nothing has to cross between parts.
Inputs may be any that keep to these rules, and one draw needn't show every extreme that they name: `lengths`: some rollout has exactly 128 cached tokens.
All inputs are finite; a program needn't handle non-finite values. No bound on the sum of `lengths` on one device may be relied on, other than what follows from the above.
Results may differ from the reference program's by a relative error of at most 0.017.
Values may be sent and summed in bfloat16 or wider, within the bound.
A program may use at most 192 MiB of HBM per device.

```python
import math
import jax
import jax.numpy as jnp
import numpy as np
from jax import lax

D = 8192
HEADS = 64
KVH = 8
HD = 128
GROUP = 8
FFW = 15360
NEW = 2
CACHE = 128
ROLLOUTS = 24
N_GX = 4


def draw_states(key, part):
    key = jax.random.fold_in(key, 11)
    key_row, key_col, key_base = jax.random.split(key, 3)
    row_scale = jnp.exp(jax.random.uniform(key_row, (ROLLOUTS, NEW, 1), jnp.float32, math.log(0.3), math.log(3.0)))
    jitter = jnp.exp(jax.random.uniform(key_col, (D,), jnp.float32, -0.5, 0.5))
    feature = jnp.arange(D, dtype=jnp.float32) / D
    ramp = jnp.sqrt(1.0 + 2.0 * feature)
    base = jnp.clip(jax.random.normal(key_base, (ROLLOUTS, NEW, D), jnp.float32), -5.0, 5.0)
    return jnp.clip(base * row_scale * ramp * jitter, -24.0, 24.0).astype(jnp.bfloat16)


def draw_key_cache(key, part):
    key = jax.random.fold_in(key, 23)
    key_base = jax.random.fold_in(key, 0)
    shape = (ROLLOUTS, CACHE, KVH, HD)
    base = jnp.clip(jax.random.normal(key_base, shape, jnp.float32), -5.0, 5.0)
    return base.astype(jnp.bfloat16)


def block_scale(rng, dims, shards, least, high):
    def one(dim, blocks):
        heights = jax.random.uniform(jax.random.fold_in(jax.random.fold_in(rng, 6), dim), (blocks,), jnp.float32, least / len(shards), high / len(shards))
        return jnp.repeat(jnp.exp(heights), dims[dim] // blocks).reshape((-1,) + (1,) * (len(dims) - dim - 1))

    level = one(*shards[0])
    for cut in shards[1:]:
        level = level * one(*cut)
    return level


def profile(count, total, most, lean):
    loads = [(1 << 20) // math.isqrt(rank ** lean) + 1 for rank in range(2, count + 1)]
    spare, given = total - most - (count - 1), [1] * (count - 1)
    while spare > 0:
        free = [i for i in range(count - 1) if given[i] < most]
        pool, budget = sum([loads[i] for i in free]), spare
        for i in free:
            more = min(most - given[i], max(1, budget * loads[i] // pool), spare)
            given[i] = given[i] + more
            spare = spare - more
    return np.array([most] + given)


def uneven_parts(own_key, amount, total, most, skew):
    if amount == 2:
        one = jax.random.randint(own_key, (), max(1, total - most), min(most, total - 1) + 1)
        return jnp.stack([one, total - one])
    tallies = jnp.asarray(profile(amount, total, most, skew), jnp.int32)
    twos = (amount - 1) // 2
    giver, receiver = tallies[1:1 + 2 * twos:2], tallies[2:2 + 2 * twos:2]
    margin = jnp.minimum(giver - 1, most - receiver)
    moved = jax.random.randint(jax.random.fold_in(own_key, 1), (twos,), 0, 1 << 20) % (margin + 1)
    tallies = tallies.at[1:1 + 2 * twos:2].set(giver - moved).at[2:2 + 2 * twos:2].set(receiver + moved)
    return tallies[jax.random.permutation(jax.random.fold_in(own_key, 2), amount)]


def bell_draw(rng, shape, spread, limit, pieces=(), held_as=jnp.bfloat16):
    loudness = block_scale(rng, shape, pieces, -0.22, 0.18) if pieces else 1.0
    drawn = jax.random.normal(rng, shape, jnp.float32) * spread * loudness
    return jnp.minimum(jnp.maximum(drawn, -limit), limit).astype(held_as)


def setup_inputs(seed: int = 0, part: int = 0) -> dict:
    seeds = jax.random.split(jax.random.key(seed), 12)
    part_keys = jax.random.split(jax.random.fold_in(seeds[11], part), 12)
    states = draw_states(jax.random.fold_in(jax.random.fold_in(seeds[11], part), 71), part)
    lengths = uneven_parts(part_keys[1], ROLLOUTS, ROLLOUTS * CACHE // 2, CACHE, 1).astype(jnp.int32)
    attn_gain = jnp.clip(1.0 + 0.15 * jax.random.normal(seeds[2], (D,), jnp.float32), 0.25, 1.75)
    mlp_gain = jnp.clip(1.0 + 0.15 * jax.random.normal(seeds[3], (D,), jnp.float32), 0.25, 1.75)
    w_qkv = bell_draw(seeds[4], (D, KVH, (GROUP + 2) * HD), D ** -0.5, 0.0625, ((0, 4), (1, 4)))
    b_qkv = bell_draw(seeds[5], (KVH, (GROUP + 2) * HD), 0.5, 3.0, ((0, 4),))
    key_cache = draw_key_cache(jax.random.fold_in(jax.random.fold_in(seeds[11], part), 71), part)
    value_cache = bell_draw(part_keys[7], (ROLLOUTS, CACHE, KVH, HD), 1.0, 6.0, ((0, 4), (2, 4)))
    w_out = bell_draw(seeds[8], (KVH, GROUP * HD, D), (HEADS * HD) ** -0.5, 0.0625, ((0, 4), (2, 4)))
    w_gate_up = bell_draw(seeds[9], (D, 2, FFW), D ** -0.5, 0.0625, ((0, 4), (2, 4)))
    w_down = bell_draw(seeds[10], (FFW, D), FFW ** -0.5, 0.046875, ((0, 4), (1, 4)))
    return {"states": states, "lengths": lengths, "attn_gain": attn_gain, "mlp_gain": mlp_gain, "w_qkv": w_qkv, "b_qkv": b_qkv, "key_cache": key_cache, "value_cache": value_cache, "w_out": w_out, "w_gate_up": w_gate_up, "w_down": w_down}


norm_eps = 1e-06
rope_base = 1000000.0

def rotate(values, position):
    half = values.shape[-1] // 2
    inverse = rope_base ** (-(jnp.arange(half, dtype=jnp.float32) * 2.0 / values.shape[-1]))
    angle = position[..., None] * inverse
    cosine = jnp.cos(angle)
    sine = jnp.sin(angle)
    first = values[..., :half]
    second = values[..., half:]
    return jnp.concatenate([first * cosine - second * sine, second * cosine + first * sine], axis=-1)

def blocked_sum(inputs, weight):
    block = inputs.shape[1] // N_GX

    def add_block(index, total):
        left = lax.dynamic_slice_in_dim(inputs, index * block, block, 1)
        right = lax.dynamic_slice_in_dim(weight, index * block, block, 0)
        partial_sum = jnp.dot(left, right, preferred_element_type=jnp.float32)
        rounded = lax.optimization_barrier(partial_sum.astype(jnp.bfloat16))
        return total + rounded.astype(jnp.float32)
    start = jnp.zeros((inputs.shape[0], weight.shape[1]), jnp.float32)
    return lax.fori_loop(0, N_GX, add_block, start)

def attend(query, keys, values, key_cache, value_cache, lengths):
    scale = 1.0 / math.sqrt(HD)
    query_f = query.astype(jnp.float32)
    old_scores = jnp.einsum('rtkgh,rckh->rkgtc', query_f, key_cache.astype(jnp.float32)) * scale
    new_scores = jnp.einsum('rtkgh,rskh->rkgts', query_f, keys.astype(jnp.float32)) * scale
    slots = jnp.arange(CACHE, dtype=jnp.int32)
    valid_old = (slots[None, :] < lengths[:, None])[:, None, None, None, :]
    order = jnp.arange(NEW, dtype=jnp.int32)
    valid_new = order[:, None] >= order[None, :]
    scores = jnp.concatenate([jnp.where(valid_old, old_scores, -1e+30), jnp.where(valid_new, new_scores, -1e+30)], axis=-1)
    highest = lax.optimization_barrier(jnp.max(scores, axis=-1, keepdims=True))
    raised = jnp.exp(scores - highest)
    weights = (raised / lax.optimization_barrier(jnp.sum(raised, axis=-1, keepdims=True))).astype(jnp.bfloat16)
    from_cache = jnp.einsum('rkgtc,rckh->rtkgh', weights[..., :CACHE].astype(jnp.float32), value_cache.astype(jnp.float32))
    from_new = jnp.einsum('rkgts,rskh->rtkgh', weights[..., CACHE:].astype(jnp.float32), values.astype(jnp.float32))
    return (from_cache + from_new).astype(jnp.bfloat16)

def reference(states, lengths, attn_gain, mlp_gain, w_qkv, b_qkv, key_cache, value_cache, w_out, w_gate_up, w_down):
    rows = ROLLOUTS * NEW
    resid = states.astype(jnp.float32).reshape(rows, D)
    mean_sq = lax.optimization_barrier(jnp.mean(resid * resid, axis=1, keepdims=True))
    normed = (resid * lax.rsqrt(mean_sq + norm_eps) * attn_gain).astype(jnp.bfloat16)
    qkv = blocked_sum(normed, w_qkv.reshape(D, KVH * (GROUP + 2) * HD))
    qkv = qkv.reshape(ROLLOUTS, NEW, KVH, GROUP + 2, HD) + b_qkv.astype(jnp.float32).reshape(KVH, GROUP + 2, HD)
    position = (lengths[:, None] + jnp.arange(NEW, dtype=jnp.int32)[None, :]).astype(jnp.float32)
    query = rotate(qkv[:, :, :, :GROUP, :], position[:, :, None, None]).astype(jnp.bfloat16)
    keys = rotate(qkv[:, :, :, GROUP, :], position[:, :, None]).astype(jnp.bfloat16)
    values = qkv[:, :, :, GROUP + 1, :].astype(jnp.bfloat16)
    heads = attend(query, keys, values, key_cache, value_cache, lengths).reshape(rows, HEADS * HD)
    mixed = resid + jnp.dot(heads, w_out.reshape(HEADS * HD, D), preferred_element_type=jnp.float32)
    mean_two = lax.optimization_barrier(jnp.mean(mixed * mixed, axis=1, keepdims=True))
    normed_two = (mixed * lax.rsqrt(mean_two + norm_eps) * mlp_gain).astype(jnp.bfloat16)
    gate_up = blocked_sum(normed_two, w_gate_up.reshape(D, 2 * FFW)).reshape(rows, 2, FFW)
    hidden = (jax.nn.silu(gate_up[:, 0]) * gate_up[:, 1]).astype(jnp.bfloat16)
    layer_out = mixed + jnp.dot(hidden, w_down, preferred_element_type=jnp.float32)
    return layer_out.reshape(ROLLOUTS, NEW, D)
```

```python
import functools
import math

import jax
import jax.numpy as jnp
from jax import lax
from jax.experimental import pallas as pl
from jax.experimental.pallas import tpu as pltpu
from jax.sharding import PartitionSpec as P

norm_eps = 1e-06
rope_base = 1000000.0
LANES = 128
MESH = pl.DeviceIdType.MESH
bf16 = jnp.bfloat16
f32 = jnp.float32


def iota(shape, dim):
    return lax.broadcasted_iota(jnp.int32, shape, dim)


def each(count, body):
    if count <= 4:
        for i in range(count):
            body(i)
    else:

        def step(i, carry):
            body(i)
            return carry

        lax.fori_loop(0, count, step, 0)


class Sizes:
    def __init__(self, nx, ny, rows, width, kv, slots, hidden, group, new):
        self.nx, self.ny, self.width, self.kv, self.slots = nx, ny, width, kv, slots
        self.hidden, self.group, self.new = hidden, group, new
        self.rl = rows // nx
        self.rb = -(-self.rl // 16) * 16
        self.rp = nx * self.rb
        self.owned = self.rl // new
        self.qw = (group + 2) * LANES
        self.qcb = self.qw // LANES
        self.hcb = hidden // LANES
        self.pair = 2 if self.hcb % 2 == 0 else 1
        per = self.hcb // self.pair
        self.cb = max(c for c in range(1, 4) if per % c == 0)
        self.cw = self.cb * LANES
        self.msgs = per // self.cb
        self.mr = -(-(self.pair * 2 * self.rl) // 16) * 16
        self.dcb = width // LANES
        self.ra = self.rp // ny
        self.reuse = min(self.qcb, self.dcb) if width * kv >= hidden else 0
        fits = 2 * kv * group * LANES >= hidden
        self.second = self.reuse + (min(self.dcb - self.reuse, self.dcb // 2) if fits else 0)


def spread(pieces, target, sz):
    m = pieces[0].shape[0]
    total = None
    for h, piece in enumerate(pieces):
        stacked = jnp.concatenate(
            [piece[:, b * LANES : (b + 1) * LANES] for b in range(sz.dcb)], axis=0
        )
        place = (iota((LANES, 2 * LANES), 1) == 2 * iota((LANES, 2 * LANES), 0) + h).astype(bf16)
        d = jnp.dot(stacked, place, preferred_element_type=f32)
        total = d if total is None else total + d
    total = total.astype(bf16)
    for b in range(sz.dcb):
        target[:, b * 2 * LANES : (b + 1) * 2 * LANES] = total[b * m : (b + 1) * m]


def kernel(
    sz,
    model_width,
    lens,
    x_ref,
    ag_ref,
    mg_ref,
    bq_ref,
    wq_hbm,
    kc_hbm,
    vc_hbm,
    wo_hbm,
    wg_hbm,
    wd_hbm,
    out_ref,
    wq,
    wo,
    wg,
    wd,
    kc,
    vc,
    lhs,
    sq,
    rq,
    ss_s,
    ss_r,
    qb,
    nk,
    nv,
    heads,
    pa,
    pr,
    pall,
    mixed,
    ts_s,
    ts_r,
    sg,
    rg,
    hid,
    dr,
    dall,
    wq_sem,
    wo_sem,
    wg_sem,
    wd_sem,
    kv_sem,
    q_ss,
    q_rs,
    s_ss,
    s_rs,
    h_ss,
    h_rs,
    a_ss,
    a_rs,
    b_ss,
    b_rs,
    t_ss,
    t_rs,
    g_ss,
    g_rs,
    u_ss,
    u_rs,
    c_ss,
    c_rs,
    d_ss,
    d_rs,
):
    nx, ny, rb, rp, kv, rl = sz.nx, sz.ny, sz.rb, sz.rp, sz.kv, sz.rl
    mx, my = lax.axis_index("gx"), lax.axis_index("gy")
    lhs_q = lhs.at[pl.ds(0, kv * rp), pl.ds(0, kv * sz.width)]
    lhs_g = lhs.at[pl.ds(0, 2 * rl * nx)]

    def px(d):
        return lax.rem(mx + d, nx)

    def py(d):
        return lax.rem(my + d, ny)

    def lane(i, n):
        return pl.ds(pl.multiple_of(i * n, n), n)

    def wq_copy(i):
        if kv == 1:
            return pltpu.make_async_copy(wq_hbm.at[:, lane(i, LANES)], wq.at[i], wq_sem.at[i])
        return pltpu.make_async_copy(wq_hbm.at[:, :, lane(i, LANES)], wq.at[i], wq_sem.at[i])

    def wq_tile(i):
        if kv == 1:
            return wq.at[i]
        return wq.at[i].reshape(kv * sz.width, LANES)

    def wg_copy(i):
        return pltpu.make_async_copy(wg_hbm.at[:, :, lane(i, LANES)], wg.at[i], wg_sem.at[i])

    def wg_tile(i):
        return wg.at[i].reshape(2 * sz.width, LANES)

    hw = kv * sz.group * LANES

    def wo_copy(i, b):
        return pltpu.make_async_copy(
            wo_hbm.at[:, lane(2 * i + b, LANES)], wo.at[i, pl.ds(b * hw, hw)], wo_sem.at[i, b]
        )

    def wd_tile(i):
        if i < sz.reuse:
            return wq_tile(i).at[pl.ds(0, sz.hidden)]
        if i < sz.second:
            return wo.at[i - sz.reuse, pl.ds(0, sz.hidden)]
        return wd.at[i - sz.second]

    def wd_copy(i):
        return pltpu.make_async_copy(
            wd_hbm.at[:, pl.ds(i * LANES, LANES)], wd_tile(i), wd_sem.at[i]
        )

    kc_copy = pltpu.make_async_copy(kc_hbm, kc, kv_sem.at[0])
    vc_copy = pltpu.make_async_copy(vc_hbm, vc, kv_sem.at[1])
    each(sz.qcb, lambda i: wq_copy(i).start())
    kc_copy.start()
    vc_copy.start()
    for b in range(2):
        each(sz.dcb // 2, lambda i: wo_copy(i, b).start())
    each(sz.hcb, lambda i: wg_copy(i).start())
    for i in range(sz.second, sz.dcb):
        wd_copy(i).start()

    barrier = pltpu.get_barrier_semaphore()

    def greet(axis, who, n):
        each(
            n - 1,
            lambda d: pl.semaphore_signal(
                barrier, inc=1, device_id={axis: who(d + 1)}, device_id_type=MESH
            ),
        )

    greet("gx", px, nx)
    greet("gy", py, ny)

    def remote(src, dst, ss, rs, axis, peer):
        return pltpu.make_async_remote_copy(
            src_ref=src, dst_ref=dst, send_sem=ss, recv_sem=rs,
            device_id={axis: peer}, device_id_type=MESH,
        )

    resid = x_ref[...].astype(f32)
    square = jnp.sum(resid * resid, axis=1, keepdims=True)
    ss_s[...] = jnp.broadcast_to(square, (rp, LANES)).reshape(nx, rb, LANES)
    xg = (resid * ag_ref[...]).astype(bf16)
    if kv == 1:
        lhs_q[...] = xg
    else:
        zero = jnp.zeros_like(xg)
        spread(
            [jnp.concatenate([xg, zero], axis=0), jnp.concatenate([zero, xg], axis=0)], lhs_q, sz
        )
    pl.semaphore_wait(barrier, nx - 1 + ny - 1)

    def s_send(d):
        p = px(d + 1)
        return remote(ss_s.at[p], ss_r.at[mx], s_ss.at[p], s_rs.at[mx], "gx", p)

    each(nx - 1, lambda d: s_send(d).start())
    ss_r[mx] = ss_s[mx]

    def qkv_cols(i, carry):
        wq_copy(2 * i).wait()
        wq_copy(2 * i + 1).wait()
        right = jnp.concatenate([wq_tile(2 * i)[...], wq_tile(2 * i + 1)[...]], axis=1)
        part = jnp.dot(lhs_q[...], right, preferred_element_type=f32).astype(bf16)
        for h in range(kv):
            at = pl.multiple_of(h * sz.qw + i * 2 * LANES, 2 * LANES)
            sq[:, :, pl.ds(at, 2 * LANES)] = part[h * rp : (h + 1) * rp].reshape(nx, rb, 2 * LANES)
        return carry

    lax.fori_loop(0, sz.qcb // 2, qkv_cols, 0)

    def q_send(d):
        p = px(d + 1)
        return remote(sq.at[p], rq.at[mx], q_ss.at[p], q_rs.at[mx], "gx", p)

    each(nx - 1, lambda d: q_send(d).start())
    for i in range(sz.reuse):
        wd_copy(i).start()

    rq[mx] = sq[mx]

    def gathered(buf_s, buf_r, ss, rs, d):
        p = px(d + 1)
        return remote(buf_s.at[p], buf_r.at[p], ss.at[p], rs.at[p], "gx", p)

    row = iota((rb, LANES), 0)
    length_row = jnp.zeros((rb, LANES), jnp.int32)
    for r in range(sz.owned):
        length_row = jnp.where(row // sz.new == r, lens[r], length_row)
    position = (length_row + row % sz.new).astype(f32)
    half = LANES // 2
    lane_i = (iota((rb, LANES), 1) % half).astype(f32)
    angle = position * jnp.exp(lane_i * (-2.0 * math.log(rope_base) / LANES))
    cosine = jnp.cos(angle)
    sine = jnp.where(iota((rb, LANES), 1) < half, -jnp.sin(angle), jnp.sin(angle))

    each(nx - 1, lambda d: gathered(ss_s, ss_r, s_ss, s_rs, d).wait_recv())
    each(nx - 1, lambda d: gathered(sq, rq, q_ss, q_rs, d).wait_recv())

    def add_up(buf, n):
        if n <= 4:
            total = buf[0].astype(f32)
            for j in range(1, n):
                total = total + buf[j].astype(f32)
            return total
        return lax.fori_loop(
            1, n, lambda j, t: t + buf[j].astype(f32), buf[0].astype(f32)
        )

    scale = lax.rsqrt(add_up(ss_r, nx)[:, :1] / model_width + norm_eps)
    qkv = add_up(rq, nx) * scale + bq_ref[...].astype(f32)

    def rotate(v):
        return (v * cosine + pltpu.roll(v, half, 1) * sine).astype(bf16)

    nk[...] = jnp.zeros_like(nk)
    nv[...] = jnp.zeros_like(nv)
    for h in range(kv):
        base = h * sz.qw
        for g in range(sz.group):
            at = (h * sz.group + g) * rb
            qb[at : at + rb] = rotate(qkv[:, base + g * LANES : base + (g + 1) * LANES])
        at = base + sz.group * LANES
        nk[h * rb : (h + 1) * rb] = rotate(qkv[:, at : at + LANES])
        nv[h * rb : (h + 1) * rb] = qkv[:, at + LANES : at + 2 * LANES].astype(bf16)

    kc_copy.wait()
    vc_copy.wait()
    old = sz.owned * sz.slots * kv

    def flat(ref):
        return ref[...] if kv == 1 else ref.reshape(old, LANES)[...]

    trans = (((1,), (1,)), ((), ()))
    query = qb[...]
    qrows = kv * sz.group * rb
    s_old = lax.dot_general(query, flat(kc), trans, preferred_element_type=f32)
    s_new = lax.dot_general(query, nk[...], trans, preferred_element_type=f32)
    rid = iota((qrows, 1), 0)
    r_head, r_roll, r_tok = rid // (sz.group * rb), (rid % rb) // sz.new, rid % sz.new
    cid = iota((1, old), 1)
    c_roll = cid // (sz.slots * kv)
    limit = jnp.zeros((1, old), jnp.int32)
    for r in range(sz.owned):
        limit = jnp.where(c_roll == r, lens[r], limit)
    c_key = jnp.where((cid // kv) % sz.slots < limit, c_roll * kv + cid % kv, -1)
    r_key = r_roll * kv + r_head
    nid = iota((1, nk.shape[0]), 1)
    n_key = jnp.where(nid < kv * rb, ((nid % rb) // sz.new) * kv + nid // rb, -1)
    inv = 1.0 / math.sqrt(LANES)
    s_old = jnp.where(r_key == c_key, s_old * inv, -1e30)
    s_new = jnp.where((r_key == n_key) & (nid % sz.new <= r_tok), s_new * inv, -1e30)
    top = jnp.maximum(
        jnp.max(s_old, axis=1, keepdims=True), jnp.max(s_new, axis=1, keepdims=True)
    )
    e_old = jnp.exp(s_old - top)
    e_new = jnp.exp(s_new - top)
    norm = 1.0 / (jnp.sum(e_old, axis=1, keepdims=True) + jnp.sum(e_new, axis=1, keepdims=True))
    attn = jnp.dot((e_old * norm).astype(bf16), flat(vc), preferred_element_type=f32)
    attn = attn + jnp.dot((e_new * norm).astype(bf16), nv[...], preferred_element_type=f32)
    attn = attn.astype(bf16)
    for b in range(kv * sz.group):
        heads[mx, :, b * LANES : (b + 1) * LANES] = attn[b * rb : (b + 1) * rb]

    def h_send(d):
        p = px(d + 1)
        return remote(heads.at[mx], heads.at[mx], h_ss.at[p], h_rs.at[mx], "gx", p)

    def h_recv(d):
        p = px(d + 1)
        return remote(heads.at[p], heads.at[p], h_ss.at[p], h_rs.at[p], "gx", p)

    each(nx - 1, lambda d: h_send(d).start())
    each(nx - 1, lambda d: h_recv(d).wait_recv())

    def all_reduce(src, got, full, ss, rs, ss2, rs2):
        def send(d):
            p = py(d + 1)
            return remote(src.at[p], got.at[my], ss.at[p], rs.at[my], "gy", p)

        def recv(d):
            p = py(d + 1)
            return remote(src.at[p], got.at[p], ss.at[p], rs.at[p], "gy", p)

        each(ny - 1, lambda d: send(d).start())
        got[my] = src[my]
        each(ny - 1, lambda d: recv(d).wait_recv())
        full[my] = add_up(got, ny).astype(bf16)

        def send2(d):
            p = py(d + 1)
            return remote(full.at[my], full.at[my], ss2.at[p], rs2.at[my], "gy", p)

        def recv2(d):
            p = py(d + 1)
            return remote(full.at[p], full.at[p], ss2.at[p], rs2.at[p], "gy", p)

        each(ny - 1, lambda d: send2(d).start())
        each(ny - 1, lambda d: recv2(d).wait_recv())
        each(ny - 1, lambda d: send(d).wait_send())
        each(ny - 1, lambda d: send2(d).wait_send())
        return full[...].astype(f32).reshape(rp, sz.width)

    step = 2 * LANES

    def out_cols(i, carry):
        left = heads[...].reshape(rp, kv * sz.group * LANES)
        wo_copy(i, 0).wait()
        wo_copy(i, 1).wait()
        right = jnp.concatenate([wo[i, 0:hw], wo[i, hw : 2 * hw]], axis=1)
        part = jnp.dot(left, right, preferred_element_type=f32)
        pa[:, :, lane(i, step)] = part.astype(bf16).reshape(ny, sz.ra, step)
        return carry

    lax.fori_loop(0, sz.width // step, out_cols, 0)
    for i in range(sz.reuse, sz.second):
        wd_copy(i).start()
    mixed[...] = x_ref[...].astype(f32) + all_reduce(pa, pr, pall, a_ss, a_rs, b_ss, b_rs)

    m = mixed[...]
    square = jnp.sum(m * m, axis=1, keepdims=True)
    ts_s[...] = jnp.broadcast_to(square, (rp, LANES)).reshape(nx, rb, LANES)

    def t_send(d):
        p = px(d + 1)
        return remote(ts_s.at[p], ts_r.at[mx], t_ss.at[p], t_rs.at[mx], "gx", p)

    each(nx - 1, lambda d: t_send(d).start())
    ts_r[mx] = ts_s[mx]
    mg = (m * mg_ref[...]).astype(bf16)
    lr = 2 * rl * nx
    want = iota((lr, rp), 0)
    have = iota((lr, rp), 1)
    inside = want % (2 * rl)
    picks = []
    for h in range(2):
        source = (want // (2 * rl)) * rb + inside - h * rl
        chosen = (have == source) & (inside >= h * rl) & (inside < (h + 1) * rl)
        picks.append(
            jnp.dot(chosen.astype(bf16), mg, preferred_element_type=f32).astype(bf16)
        )
    spread(picks, lhs_g, sz)

    def gate_cols(i, carry):
        parts = []
        for a in range(sz.pair):
            for c in range(sz.cb):
                wg_copy((i * sz.pair + a) * sz.cb + c).wait()
        for a in range(sz.pair):
            first = (i * sz.pair + a) * sz.cb
            right = jnp.concatenate([wg_tile(first + c)[...] for c in range(sz.cb)], axis=1)
            parts.append(jnp.dot(lhs_g[...], right, preferred_element_type=f32))
        for j in range(nx):
            rows = [part[j * 2 * rl : (j + 1) * 2 * rl] for part in parts]
            spare = sz.mr - sz.pair * 2 * rl
            if spare:
                rows.append(jnp.zeros((spare, sz.cw), f32))
            sg[i, j] = jnp.concatenate(rows, axis=0).astype(bf16)

        def send(d):
            p = px(d + 1)
            remote(
                sg.at[i, p], rg.at[i, mx], g_ss.at[i, p], g_rs.at[i, mx], "gx", p
            ).start()

        each(nx - 1, send)
        rg[i, mx] = sg[i, mx]
        return carry

    lax.fori_loop(0, sz.msgs, gate_cols, 0)

    def t_recv(d):
        p = px(d + 1)
        return remote(ts_s.at[p], ts_r.at[p], t_ss.at[p], t_rs.at[p], "gx", p)

    each(nx - 1, lambda d: t_recv(d).wait_recv())
    scale_two = lax.rsqrt(add_up(ts_r, nx)[:, :1] / model_width + norm_eps)

    def hid_send(i, d):
        p = px(d + 1)
        cols = hid.at[i, mx]
        return remote(cols, cols, u_ss.at[i, p], u_rs.at[i, mx], "gx", p)

    def hid_recv(i, d):
        p = px(d + 1)
        cols = hid.at[i, p]
        return remote(cols, cols, u_ss.at[i, p], u_rs.at[i, p], "gx", p)

    def act_cols(i, carry):
        def arrive(d):
            p = px(d + 1)
            remote(
                sg.at[i, p], rg.at[i, p], g_ss.at[i, p], g_rs.at[i, p], "gx", p
            ).wait_recv()

        each(nx - 1, arrive)
        total = add_up(rg.at[i], nx)
        total = jnp.concatenate([total, jnp.zeros((rb, sz.cw), f32)], axis=0)
        for a in range(sz.pair):
            at = a * 2 * rl
            gate = total[at : at + rb] * scale_two
            up = total[at + rl : at + rl + rb] * scale_two
            value = gate / (1.0 + jnp.exp(-gate)) * up
            hid[i, mx, :, a * sz.cw : (a + 1) * sz.cw] = value.astype(bf16)
        each(nx - 1, lambda d: hid_send(i, d).start())
        return carry

    lax.fori_loop(0, sz.msgs, act_cols, 0)
    for i in range(sz.dcb):
        wd_copy(i).wait()

    def hid_wait(i, carry):
        each(nx - 1, lambda d: hid_recv(i, d).wait_recv())
        return carry

    lax.fori_loop(0, sz.msgs, hid_wait, 0)
    span = sz.pair * sz.cw
    for i in range(sz.dcb // 2):
        part = None
        for k in range(sz.msgs):
            right = jnp.concatenate(
                [wd_tile(2 * i + b)[k * span : (k + 1) * span] for b in range(2)], axis=1
            )
            d = jnp.dot(hid[k].reshape(rp, span), right, preferred_element_type=f32)
            part = d if part is None else part + d
        pa[:, :, i * step : (i + 1) * step] = part.astype(bf16).reshape(ny, sz.ra, step)
    out_ref[...] = mixed[...] + all_reduce(pa, dr, dall, c_ss, c_rs, d_ss, d_rs)

    each(nx - 1, lambda d: s_send(d).wait_send())
    each(nx - 1, lambda d: q_send(d).wait_send())
    each(nx - 1, lambda d: h_send(d).wait_send())
    each(nx - 1, lambda d: t_send(d).wait_send())

    def sent(i, carry):
        def one(d):
            p = px(d + 1)
            remote(
                sg.at[i, p], rg.at[i, mx], g_ss.at[i, p], g_rs.at[i, mx], "gx", p
            ).wait_send()
            hid_send(i, d).wait_send()

        each(nx - 1, one)
        return carry

    lax.fori_loop(0, sz.msgs, sent, 0)


def on_device(
    states,
    lengths,
    attn_gain,
    mlp_gain,
    w_qkv,
    b_qkv,
    key_cache,
    value_cache,
    w_out,
    w_gate_up,
    w_down,
):
    nx, ny = lax.axis_size("gx"), lax.axis_size("gy")
    rollouts, new, width = states.shape
    owned, slots, kv, head = key_cache.shape
    group = w_qkv.shape[2] // head - 2
    hidden = w_gate_up.shape[2]
    sz = Sizes(nx, ny, rollouts * new, width, kv, slots, hidden, group, new)
    x = jnp.pad(
        states.reshape(nx, sz.rl, width), ((0, 0), (0, sz.rb - sz.rl), (0, 0))
    ).reshape(sz.rp, width)
    bias = b_qkv.reshape(1, kv * sz.qw)
    inner = (kv,) if kv > 1 else ()
    kcache = key_cache.reshape((owned * slots,) + inner + (head,))
    vcache = value_cache.reshape((owned * slots,) + inner + (head,))
    wq = w_qkv.reshape((width,) + inner + (sz.qw,))
    wo = w_out.reshape(kv * group * head, width)
    dma = pltpu.SemaphoreType.DMA
    vm = pltpu.VMEM
    heads_w = kv * group * head
    newk = -(-kv * sz.rb // LANES) * LANES
    scratch = [
        vm((sz.qcb, width) + inner + (LANES,), bf16),
        vm((sz.dcb // 2, 2 * heads_w, LANES), bf16),
        vm((sz.hcb, width, 2, LANES), bf16),
        vm((max(1, sz.dcb - sz.second), hidden if sz.second < sz.dcb else 16, LANES), bf16),
        vm(kcache.shape, bf16),
        vm(vcache.shape, bf16),
        vm((max(kv * sz.rp, 2 * sz.rl * nx), 2 * width), bf16),
        vm((nx, sz.rb, kv * sz.qw), bf16),
        vm((nx, sz.rb, kv * sz.qw), bf16),
        vm((nx, sz.rb, LANES), f32),
        vm((nx, sz.rb, LANES), f32),
        vm((kv * group * sz.rb, LANES), bf16),
        vm((newk, LANES), bf16),
        vm((newk, LANES), bf16),
        vm((nx, sz.rb, heads_w), bf16),
        vm((ny, sz.ra, width), bf16),
        vm((ny, sz.ra, width), bf16),
        vm((ny, sz.ra, width), bf16),
        vm((sz.rp, width), f32),
        vm((nx, sz.rb, LANES), f32),
        vm((nx, sz.rb, LANES), f32),
        vm((sz.msgs, nx, sz.mr, sz.cw), bf16),
        vm((sz.msgs, nx, sz.mr, sz.cw), bf16),
        vm((sz.msgs, nx, sz.rb, sz.pair * sz.cw), bf16),
        vm((ny, sz.ra, width), bf16),
        vm((ny, sz.ra, width), bf16),
        dma((sz.qcb,)),
        dma((sz.dcb // 2, 2)),
        dma((sz.hcb,)),
        dma((sz.dcb,)),
        dma((2,)),
    ]
    scratch += [dma((nx,))] * 6 + [dma((ny,))] * 4 + [dma((nx,))] * 2
    scratch += [dma((sz.msgs, nx))] * 4 + [dma((ny,))] * 4
    anyspec = pl.BlockSpec(memory_space=pl.ANY)
    vspec = pl.BlockSpec(memory_space=pltpu.VMEM)
    out = pl.pallas_call(
        functools.partial(kernel, sz, width * nx),
        out_shape=jax.ShapeDtypeStruct((sz.rp, width), f32),
        in_specs=[pl.BlockSpec(memory_space=pltpu.SMEM)] + [vspec] * 4 + [anyspec] * 6,
        out_specs=vspec,
        scratch_shapes=scratch,
        compiler_params=pltpu.CompilerParams(
            collective_id=0, has_side_effects=True, vmem_limit_bytes=63 * 2**20
        ),
    )(
        lengths,
        x,
        attn_gain.reshape(1, width),
        mlp_gain.reshape(1, width),
        bias,
        wq,
        kcache,
        vcache,
        wo,
        w_gate_up,
        w_down,
    )
    out = out.reshape(nx, sz.rb, width)[:, : sz.rl]
    return out.reshape(rollouts, new, width)


def solution(mesh):
    in_specs = (
        P("groups", None, "gx"),
        P(("groups", "gx")),
        P("gx"),
        P("gx"),
        P("gx", "gy", None),
        P("gy", None),
        P(("groups", "gx"), None, "gy", None),
        P(("groups", "gx"), None, "gy", None),
        P("gy", None, "gx"),
        P("gx", None, "gy"),
        P("gy", "gx"),
    )
    out_specs = P("groups", None, "gx")
    return jax.shard_map(
        on_device, mesh=mesh, in_specs=in_specs, out_specs=out_specs, check_vma=False
    )
```

```python
import functools
import math

import jax
import jax.numpy as jnp
from jax import lax
from jax.experimental import pallas as pl
from jax.experimental.pallas import tpu as pltpu
from jax.sharding import PartitionSpec as P

norm_eps = 1e-06
rope_base = 1000000.0
LANES = 128
MESH = pl.DeviceIdType.MESH
bf16 = jnp.bfloat16
f32 = jnp.float32


def iota(shape, dim):
    return lax.broadcasted_iota(jnp.int32, shape, dim)


def each(count, body):
    if count <= 4:
        for i in range(count):
            body(i)
    else:

        def step(i, carry):
            body(i)
            return carry

        lax.fori_loop(0, count, step, 0)


class Sizes:
    def __init__(self, nx, ny, rows, width, kv, slots, hidden, group, new):
        self.nx, self.ny, self.width, self.kv, self.slots = nx, ny, width, kv, slots
        self.hidden, self.group, self.new = hidden, group, new
        self.rl = rows // nx
        self.rb = -(-self.rl // 16) * 16
        self.rp = nx * self.rb
        self.owned = self.rl // new
        self.qw = (group + 2) * LANES
        self.qcb = self.qw // LANES
        self.hcb = hidden // LANES
        self.pair = 2 if self.hcb % 2 == 0 else 1
        per = self.hcb // self.pair
        self.cb = max(c for c in range(1, 4) if per % c == 0)
        self.cw = self.cb * LANES
        self.msgs = per // self.cb
        self.mr = -(-(self.pair * 2 * self.rl) // 16) * 16
        self.dcb = width // LANES
        self.ra = self.rp // ny
        self.reuse = min(self.qcb, self.dcb) if width * kv >= hidden else 0
        fits = 2 * kv * group * LANES >= hidden
        self.second = self.reuse + (min(self.dcb - self.reuse, self.dcb // 2) if fits else 0)


def spread(pieces, target, sz):
    m = pieces[0].shape[0]
    total = None
    for h, piece in enumerate(pieces):
        stacked = jnp.concatenate(
            [piece[:, b * LANES : (b + 1) * LANES] for b in range(sz.dcb)], axis=0
        )
        place = (iota((LANES, 2 * LANES), 1) == 2 * iota((LANES, 2 * LANES), 0) + h).astype(bf16)
        d = jnp.dot(stacked, place, preferred_element_type=f32)
        total = d if total is None else total + d
    total = total.astype(bf16)
    for b in range(sz.dcb):
        target[:, b * 2 * LANES : (b + 1) * 2 * LANES] = total[b * m : (b + 1) * m]


def kernel(
    sz,
    model_width,
    lens,
    x_ref,
    ag_ref,
    mg_ref,
    bq_ref,
    wq_hbm,
    kc_hbm,
    vc_hbm,
    wo_hbm,
    wg_hbm,
    wd_hbm,
    out_ref,
    wq,
    wo,
    wg,
    wd,
    kc,
    vc,
    lhs,
    sq,
    rq,
    ss_s,
    ss_r,
    qb,
    nk,
    nv,
    heads,
    pa,
    pr,
    pall,
    mixed,
    ts_s,
    ts_r,
    sg,
    rg,
    hid,
    dr,
    dall,
    wq_sem,
    wo_sem,
    wg_sem,
    wd_sem,
    kv_sem,
    q_ss,
    q_rs,
    s_ss,
    s_rs,
    h_ss,
    h_rs,
    a_ss,
    a_rs,
    b_ss,
    b_rs,
    t_ss,
    t_rs,
    g_ss,
    g_rs,
    u_ss,
    u_rs,
    c_ss,
    c_rs,
    d_ss,
    d_rs,
):
    nx, ny, rb, rp, kv, rl = sz.nx, sz.ny, sz.rb, sz.rp, sz.kv, sz.rl
    mx, my = lax.axis_index("gx"), lax.axis_index("gy")
    lhs_q = lhs.at[pl.ds(0, kv * rp), pl.ds(0, kv * sz.width)]
    lhs_g = lhs.at[pl.ds(0, 2 * rl * nx)]

    def px(d):
        return lax.rem(mx + d, nx)

    def py(d):
        return lax.rem(my + d, ny)

    def lane(i, n):
        return pl.ds(pl.multiple_of(i * n, n), n)

    def wq_copy(i):
        if kv == 1:
            return pltpu.make_async_copy(wq_hbm.at[:, lane(i, LANES)], wq.at[i], wq_sem.at[i])
        return pltpu.make_async_copy(wq_hbm.at[:, :, lane(i, LANES)], wq.at[i], wq_sem.at[i])

    def wq_tile(i):
        if kv == 1:
            return wq.at[i]
        return wq.at[i].reshape(kv * sz.width, LANES)

    def wg_copy(i):
        return pltpu.make_async_copy(wg_hbm.at[:, :, lane(i, LANES)], wg.at[i], wg_sem.at[i])

    def wg_tile(i):
        return wg.at[i].reshape(2 * sz.width, LANES)

    hw = kv * sz.group * LANES

    def wo_copy(i, b):
        return pltpu.make_async_copy(
            wo_hbm.at[:, lane(2 * i + b, LANES)], wo.at[i, pl.ds(b * hw, hw)], wo_sem.at[i, b]
        )

    def wd_tile(i):
        if i < sz.reuse:
            return wq_tile(i).at[pl.ds(0, sz.hidden)]
        if i < sz.second:
            return wo.at[i - sz.reuse, pl.ds(0, sz.hidden)]
        return wd.at[i - sz.second]

    def wd_copy(i):
        return pltpu.make_async_copy(
            wd_hbm.at[:, pl.ds(i * LANES, LANES)], wd_tile(i), wd_sem.at[i]
        )

    kc_copy = pltpu.make_async_copy(kc_hbm, kc, kv_sem.at[0])
    vc_copy = pltpu.make_async_copy(vc_hbm, vc, kv_sem.at[1])
    each(sz.qcb, lambda i: wq_copy(i).start())
    kc_copy.start()
    vc_copy.start()
    for b in range(2):
        each(sz.dcb // 2, lambda i: wo_copy(i, b).start())
    each(sz.hcb, lambda i: wg_copy(i).start())
    for i in range(sz.second, sz.dcb):
        wd_copy(i).start()

    barrier = pltpu.get_barrier_semaphore()

    def greet(axis, who, n):
        each(
            n - 1,
            lambda d: pl.semaphore_signal(
                barrier, inc=1, device_id={axis: who(d + 1)}, device_id_type=MESH
            ),
        )

    greet("gx", px, nx)
    greet("gy", py, ny)

    def remote(src, dst, ss, rs, axis, peer):
        return pltpu.make_async_remote_copy(
            src_ref=src, dst_ref=dst, send_sem=ss, recv_sem=rs,
            device_id={axis: peer}, device_id_type=MESH,
        )

    resid = x_ref[...].astype(f32)
    square = jnp.sum(resid * resid, axis=1, keepdims=True)
    ss_s[...] = jnp.broadcast_to(square, (rp, LANES)).reshape(nx, rb, LANES)
    xg = (resid * ag_ref[...]).astype(bf16)
    if kv == 1:
        lhs_q[...] = xg
    else:
        zero = jnp.zeros_like(xg)
        spread(
            [jnp.concatenate([xg, zero], axis=0), jnp.concatenate([zero, xg], axis=0)], lhs_q, sz
        )
    pl.semaphore_wait(barrier, nx - 1 + ny - 1)

    def s_send(d):
        p = px(d + 1)
        return remote(ss_s.at[p], ss_r.at[mx], s_ss.at[p], s_rs.at[mx], "gx", p)

    each(nx - 1, lambda d: s_send(d).start())
    ss_r[mx] = ss_s[mx]

    def qkv_cols(i, carry):
        wq_copy(2 * i).wait()
        wq_copy(2 * i + 1).wait()
        right = jnp.concatenate([wq_tile(2 * i)[...], wq_tile(2 * i + 1)[...]], axis=1)
        part = jnp.dot(lhs_q[...], right, preferred_element_type=f32).astype(bf16)
        for h in range(kv):
            sq[i, :, :, h * 2 * LANES : (h + 1) * 2 * LANES] = part[
                h * rp : (h + 1) * rp
            ].reshape(nx, rb, 2 * LANES)
        each(nx - 1, lambda d: q_send(i, d).start())
        rq[i, mx] = sq[i, mx]
        return carry

    def q_send(i, d):
        p = px(d + 1)
        return remote(sq.at[i, p], rq.at[i, mx], q_ss.at[i, p], q_rs.at[i, mx], "gx", p)

    def q_recv(i, d):
        p = px(d + 1)
        return remote(sq.at[i, p], rq.at[i, p], q_ss.at[i, p], q_rs.at[i, p], "gx", p)

    def over_chunks(body):
        def step(i, carry):
            each(nx - 1, lambda d: body(i, d))
            return carry

        lax.fori_loop(0, sz.qcb // 2, step, 0)

    lax.fori_loop(0, sz.qcb // 2, qkv_cols, 0)

    for i in range(sz.reuse):
        wd_copy(i).start()

    def gathered(buf_s, buf_r, ss, rs, d):
        p = px(d + 1)
        return remote(buf_s.at[p], buf_r.at[p], ss.at[p], rs.at[p], "gx", p)

    row = iota((rb, LANES), 0)
    length_row = jnp.zeros((rb, LANES), jnp.int32)
    for r in range(sz.owned):
        length_row = jnp.where(row // sz.new == r, lens[r], length_row)
    position = (length_row + row % sz.new).astype(f32)
    half = LANES // 2
    lane_i = (iota((rb, LANES), 1) % half).astype(f32)
    angle = position * jnp.exp(lane_i * (-2.0 * math.log(rope_base) / LANES))
    cosine = jnp.cos(angle)
    sine = jnp.where(iota((rb, LANES), 1) < half, -jnp.sin(angle), jnp.sin(angle))

    each(nx - 1, lambda d: gathered(ss_s, ss_r, s_ss, s_rs, d).wait_recv())
    over_chunks(lambda i, d: q_recv(i, d).wait_recv())

    def add_up(buf, n):
        if n <= 4:
            total = buf[0].astype(f32)
            for j in range(1, n):
                total = total + buf[j].astype(f32)
            return total
        return lax.fori_loop(
            1, n, lambda j, t: t + buf[j].astype(f32), buf[0].astype(f32)
        )

    scale = lax.rsqrt(add_up(ss_r, nx)[:, :1] / model_width + norm_eps)
    sums = [add_up(rq.at[i], nx) for i in range(sz.qcb // 2)]
    sums = [t[:, h * 2 * LANES : (h + 1) * 2 * LANES] for h in range(kv) for t in sums]
    qkv = jnp.concatenate(sums, axis=1) * scale + bq_ref[...].astype(f32)

    def rotate(v):
        return (v * cosine + pltpu.roll(v, half, 1) * sine).astype(bf16)

    nk[...] = jnp.zeros_like(nk)
    nv[...] = jnp.zeros_like(nv)
    for h in range(kv):
        base = h * sz.qw
        for g in range(sz.group):
            at = (h * sz.group + g) * rb
            qb[at : at + rb] = rotate(qkv[:, base + g * LANES : base + (g + 1) * LANES])
        at = base + sz.group * LANES
        nk[h * rb : (h + 1) * rb] = rotate(qkv[:, at : at + LANES])
        nv[h * rb : (h + 1) * rb] = qkv[:, at + LANES : at + 2 * LANES].astype(bf16)

    kc_copy.wait()
    vc_copy.wait()
    old = sz.owned * sz.slots * kv

    def flat(ref):
        return ref[...] if kv == 1 else ref.reshape(old, LANES)[...]

    trans = (((1,), (1,)), ((), ()))
    query = qb[...]
    qrows = kv * sz.group * rb
    s_old = lax.dot_general(query, flat(kc), trans, preferred_element_type=f32)
    s_new = lax.dot_general(query, nk[...], trans, preferred_element_type=f32)
    rid = iota((qrows, 1), 0)
    r_head, r_roll, r_tok = rid // (sz.group * rb), (rid % rb) // sz.new, rid % sz.new
    cid = iota((1, old), 1)
    c_roll = cid // (sz.slots * kv)
    limit = jnp.zeros((1, old), jnp.int32)
    for r in range(sz.owned):
        limit = jnp.where(c_roll == r, lens[r], limit)
    c_key = jnp.where((cid // kv) % sz.slots < limit, c_roll * kv + cid % kv, -1)
    r_key = r_roll * kv + r_head
    nid = iota((1, nk.shape[0]), 1)
    n_key = jnp.where(nid < kv * rb, ((nid % rb) // sz.new) * kv + nid // rb, -1)
    inv = 1.0 / math.sqrt(LANES)
    s_old = jnp.where(r_key == c_key, s_old * inv, -1e30)
    s_new = jnp.where((r_key == n_key) & (nid % sz.new <= r_tok), s_new * inv, -1e30)
    top = jnp.maximum(
        jnp.max(s_old, axis=1, keepdims=True), jnp.max(s_new, axis=1, keepdims=True)
    )
    e_old = jnp.exp(s_old - top)
    e_new = jnp.exp(s_new - top)
    norm = 1.0 / (jnp.sum(e_old, axis=1, keepdims=True) + jnp.sum(e_new, axis=1, keepdims=True))
    attn = jnp.dot((e_old * norm).astype(bf16), flat(vc), preferred_element_type=f32)
    attn = attn + jnp.dot((e_new * norm).astype(bf16), nv[...], preferred_element_type=f32)
    attn = attn.astype(bf16)
    for b in range(kv * sz.group):
        heads[mx, :, b * LANES : (b + 1) * LANES] = attn[b * rb : (b + 1) * rb]

    def h_send(d):
        p = px(d + 1)
        return remote(heads.at[mx], heads.at[mx], h_ss.at[p], h_rs.at[mx], "gx", p)

    def h_recv(d):
        p = px(d + 1)
        return remote(heads.at[p], heads.at[p], h_ss.at[p], h_rs.at[p], "gx", p)

    each(nx - 1, lambda d: h_send(d).start())
    each(nx - 1, lambda d: h_recv(d).wait_recv())

    def all_reduce(src, got, full, ss, rs, ss2, rs2):
        def send(d):
            p = py(d + 1)
            return remote(src.at[p], got.at[my], ss.at[p], rs.at[my], "gy", p)

        def recv(d):
            p = py(d + 1)
            return remote(src.at[p], got.at[p], ss.at[p], rs.at[p], "gy", p)

        each(ny - 1, lambda d: send(d).start())
        got[my] = src[my]
        each(ny - 1, lambda d: recv(d).wait_recv())
        full[my] = add_up(got, ny).astype(bf16)

        def send2(d):
            p = py(d + 1)
            return remote(full.at[my], full.at[my], ss2.at[p], rs2.at[my], "gy", p)

        def recv2(d):
            p = py(d + 1)
            return remote(full.at[p], full.at[p], ss2.at[p], rs2.at[p], "gy", p)

        each(ny - 1, lambda d: send2(d).start())
        each(ny - 1, lambda d: recv2(d).wait_recv())
        each(ny - 1, lambda d: send(d).wait_send())
        each(ny - 1, lambda d: send2(d).wait_send())
        return full[...].astype(f32).reshape(rp, sz.width)

    step = 2 * LANES

    def out_cols(i, carry):
        left = heads[...].reshape(rp, kv * sz.group * LANES)
        wo_copy(i, 0).wait()
        wo_copy(i, 1).wait()
        right = jnp.concatenate([wo[i, 0:hw], wo[i, hw : 2 * hw]], axis=1)
        part = jnp.dot(left, right, preferred_element_type=f32)
        pa[:, :, lane(i, step)] = part.astype(bf16).reshape(ny, sz.ra, step)
        return carry

    lax.fori_loop(0, sz.width // step, out_cols, 0)
    for i in range(sz.reuse, sz.second):
        wd_copy(i).start()
    mixed[...] = x_ref[...].astype(f32) + all_reduce(pa, pr, pall, a_ss, a_rs, b_ss, b_rs)

    m = mixed[...]
    square = jnp.sum(m * m, axis=1, keepdims=True)
    ts_s[...] = jnp.broadcast_to(square, (rp, LANES)).reshape(nx, rb, LANES)

    def t_send(d):
        p = px(d + 1)
        return remote(ts_s.at[p], ts_r.at[mx], t_ss.at[p], t_rs.at[mx], "gx", p)

    each(nx - 1, lambda d: t_send(d).start())
    ts_r[mx] = ts_s[mx]
    mg = (m * mg_ref[...]).astype(bf16)
    lr = 2 * rl * nx
    want = iota((lr, rp), 0)
    have = iota((lr, rp), 1)
    inside = want % (2 * rl)
    picks = []
    for h in range(2):
        source = (want // (2 * rl)) * rb + inside - h * rl
        chosen = (have == source) & (inside >= h * rl) & (inside < (h + 1) * rl)
        picks.append(
            jnp.dot(chosen.astype(bf16), mg, preferred_element_type=f32).astype(bf16)
        )
    spread(picks, lhs_g, sz)

    def gate_cols(i, carry):
        parts = []
        for a in range(sz.pair):
            for c in range(sz.cb):
                wg_copy((i * sz.pair + a) * sz.cb + c).wait()
        first = i * sz.pair * sz.cb
        right = jnp.concatenate(
            [wg_tile(first + c)[...] for c in range(sz.pair * sz.cb)], axis=1
        )
        both = jnp.dot(lhs_g[...], right, preferred_element_type=f32)
        for a in range(sz.pair):
            parts.append(both[:, a * sz.cw : (a + 1) * sz.cw])
        for j in range(nx):
            rows = [part[j * 2 * rl : (j + 1) * 2 * rl] for part in parts]
            spare = sz.mr - sz.pair * 2 * rl
            if spare:
                rows.append(jnp.zeros((spare, sz.cw), f32))
            sg[i, j] = jnp.concatenate(rows, axis=0).astype(bf16)

        def send(d):
            p = px(d + 1)
            remote(
                sg.at[i, p], rg.at[i, mx], g_ss.at[i, p], g_rs.at[i, mx], "gx", p
            ).start()

        each(nx - 1, send)
        rg[i, mx] = sg[i, mx]
        return carry

    lax.fori_loop(0, sz.msgs, gate_cols, 0)

    def t_recv(d):
        p = px(d + 1)
        return remote(ts_s.at[p], ts_r.at[p], t_ss.at[p], t_rs.at[p], "gx", p)

    each(nx - 1, lambda d: t_recv(d).wait_recv())
    scale_two = lax.rsqrt(add_up(ts_r, nx)[:, :1] / model_width + norm_eps)

    def hid_send(i, d):
        p = px(d + 1)
        cols = hid.at[i, mx]
        return remote(cols, cols, u_ss.at[i, p], u_rs.at[i, mx], "gx", p)

    def hid_recv(i, d):
        p = px(d + 1)
        cols = hid.at[i, p]
        return remote(cols, cols, u_ss.at[i, p], u_rs.at[i, p], "gx", p)

    def act_cols(i, carry):
        def arrive(d):
            p = px(d + 1)
            remote(
                sg.at[i, p], rg.at[i, p], g_ss.at[i, p], g_rs.at[i, p], "gx", p
            ).wait_recv()

        each(nx - 1, arrive)
        total = add_up(rg.at[i], nx)
        total = jnp.concatenate([total, jnp.zeros((rb, sz.cw), f32)], axis=0)
        for a in range(sz.pair):
            at = a * 2 * rl
            gate = total[at : at + rb] * scale_two
            up = total[at + rl : at + rl + rb] * scale_two
            value = gate / (1.0 + jnp.exp(-gate)) * up
            hid[i, mx, :, a * sz.cw : (a + 1) * sz.cw] = value.astype(bf16)
        each(nx - 1, lambda d: hid_send(i, d).start())
        return carry

    lax.fori_loop(0, sz.msgs, act_cols, 0)
    for i in range(sz.dcb):
        wd_copy(i).wait()

    def hid_wait(i, carry):
        each(nx - 1, lambda d: hid_recv(i, d).wait_recv())
        return carry

    lax.fori_loop(0, sz.msgs, hid_wait, 0)
    span = sz.pair * sz.cw
    for i in range(sz.dcb // 2):
        part = None
        for k in range(sz.msgs):
            right = jnp.concatenate(
                [wd_tile(2 * i + b)[k * span : (k + 1) * span] for b in range(2)], axis=1
            )
            d = jnp.dot(hid[k].reshape(rp, span), right, preferred_element_type=f32)
            part = d if part is None else part + d
        pa[:, :, i * step : (i + 1) * step] = part.astype(bf16).reshape(ny, sz.ra, step)
    out_ref[...] = mixed[...] + all_reduce(pa, dr, dall, c_ss, c_rs, d_ss, d_rs)

    each(nx - 1, lambda d: s_send(d).wait_send())
    over_chunks(lambda i, d: q_send(i, d).wait_send())
    each(nx - 1, lambda d: h_send(d).wait_send())
    each(nx - 1, lambda d: t_send(d).wait_send())

    def sent(i, carry):
        def one(d):
            p = px(d + 1)
            remote(
                sg.at[i, p], rg.at[i, mx], g_ss.at[i, p], g_rs.at[i, mx], "gx", p
            ).wait_send()
            hid_send(i, d).wait_send()

        each(nx - 1, one)
        return carry

    lax.fori_loop(0, sz.msgs, sent, 0)


def on_device(
    states,
    lengths,
    attn_gain,
    mlp_gain,
    w_qkv,
    b_qkv,
    key_cache,
    value_cache,
    w_out,
    w_gate_up,
    w_down,
):
    nx, ny = lax.axis_size("gx"), lax.axis_size("gy")
    rollouts, new, width = states.shape
    owned, slots, kv, head = key_cache.shape
    group = w_qkv.shape[2] // head - 2
    hidden = w_gate_up.shape[2]
    sz = Sizes(nx, ny, rollouts * new, width, kv, slots, hidden, group, new)
    x = jnp.pad(
        states.reshape(nx, sz.rl, width), ((0, 0), (0, sz.rb - sz.rl), (0, 0))
    ).reshape(sz.rp, width)
    bias = b_qkv.reshape(1, kv * sz.qw)
    inner = (kv,) if kv > 1 else ()
    kcache = key_cache.reshape((owned * slots,) + inner + (head,))
    vcache = value_cache.reshape((owned * slots,) + inner + (head,))
    wq = w_qkv.reshape((width,) + inner + (sz.qw,))
    wo = w_out.reshape(kv * group * head, width)
    dma = pltpu.SemaphoreType.DMA
    vm = pltpu.VMEM
    heads_w = kv * group * head
    newk = -(-kv * sz.rb // LANES) * LANES
    scratch = [
        vm((sz.qcb, width) + inner + (LANES,), bf16),
        vm((sz.dcb // 2, 2 * heads_w, LANES), bf16),
        vm((sz.hcb, width, 2, LANES), bf16),
        vm((max(1, sz.dcb - sz.second), hidden if sz.second < sz.dcb else 16, LANES), bf16),
        vm(kcache.shape, bf16),
        vm(vcache.shape, bf16),
        vm((max(kv * sz.rp, 2 * sz.rl * nx), 2 * width), bf16),
        vm((sz.qcb // 2, nx, sz.rb, kv * 2 * LANES), bf16),
        vm((sz.qcb // 2, nx, sz.rb, kv * 2 * LANES), bf16),
        vm((nx, sz.rb, LANES), f32),
        vm((nx, sz.rb, LANES), f32),
        vm((kv * group * sz.rb, LANES), bf16),
        vm((newk, LANES), bf16),
        vm((newk, LANES), bf16),
        vm((nx, sz.rb, heads_w), bf16),
        vm((ny, sz.ra, width), bf16),
        vm((ny, sz.ra, width), bf16),
        vm((ny, sz.ra, width), bf16),
        vm((sz.rp, width), f32),
        vm((nx, sz.rb, LANES), f32),
        vm((nx, sz.rb, LANES), f32),
        vm((sz.msgs, nx, sz.mr, sz.cw), bf16),
        vm((sz.msgs, nx, sz.mr, sz.cw), bf16),
        vm((sz.msgs, nx, sz.rb, sz.pair * sz.cw), bf16),
        vm((ny, sz.ra, width), bf16),
        vm((ny, sz.ra, width), bf16),
        dma((sz.qcb,)),
        dma((sz.dcb // 2, 2)),
        dma((sz.hcb,)),
        dma((sz.dcb,)),
        dma((2,)),
    ]
    scratch += [dma((sz.qcb // 2, nx))] * 2 + [dma((nx,))] * 4 + [dma((ny,))] * 4 + [dma((nx,))] * 2
    scratch += [dma((sz.msgs, nx))] * 4 + [dma((ny,))] * 4
    anyspec = pl.BlockSpec(memory_space=pl.ANY)
    vspec = pl.BlockSpec(memory_space=pltpu.VMEM)
    out = pl.pallas_call(
        functools.partial(kernel, sz, width * nx),
        out_shape=jax.ShapeDtypeStruct((sz.rp, width), f32),
        in_specs=[pl.BlockSpec(memory_space=pltpu.SMEM)] + [vspec] * 4 + [anyspec] * 6,
        out_specs=vspec,
        scratch_shapes=scratch,
        compiler_params=pltpu.CompilerParams(
            collective_id=0, has_side_effects=True, vmem_limit_bytes=63 * 2**20
        ),
    )(
        lengths,
        x,
        attn_gain.reshape(1, width),
        mlp_gain.reshape(1, width),
        bias,
        wq,
        kcache,
        vcache,
        wo,
        w_gate_up,
        w_down,
    )
    out = out.reshape(nx, sz.rb, width)[:, : sz.rl]
    return out.reshape(rollouts, new, width)


def solution(mesh):
    in_specs = (
        P("groups", None, "gx"),
        P(("groups", "gx")),
        P("gx"),
        P("gx"),
        P("gx", "gy", None),
        P("gy", None),
        P(("groups", "gx"), None, "gy", None),
        P(("groups", "gx"), None, "gy", None),
        P("gy", None, "gx"),
        P("gx", None, "gy"),
        P("gy", "gx"),
    )
    out_specs = P("groups", None, "gx")
    return jax.shard_map(
        on_device, mesh=mesh, in_specs=in_specs, out_specs=out_specs, check_vma=False
    )
```
